1024 devices in a mesh: node: 64 (over y, x, core), local: 16 (over z).
Axes of the slice: x: 4, y: 8, z: 16, core: 2. Of those that a mesh axis runs over, the one named last changes fastest.
Arguments:
- d_out: bfloat16 [4096, 6144], P('local', 'node'), may hold values from -2.5 to 2.5
- node_ids: int32 [4096, 4], P('local'), may hold values from 0 to 63, as said below
- gates: float32 [64, 16, 32, 2], P('node'), may hold values from 0.1 to 1
- hidden: bfloat16 [64, 16, 32, 2, 1024], P('node', None, None, None, 'local'), may hold values from -2.5 to 2.5
- w_down: bfloat16 [128, 1024, 6144], P('node', 'local'), may hold values from -0.1875 to 0.1875
Outputs:
- d_hidden: bfloat16 [64, 16, 32, 2, 1024], P('node', None, None, None, 'local')
- d_down: bfloat16 [128, 1024, 6144], P('node', 'local')
- d_gates: float32 [4096, 4, 2], P('local')
The draws below stay inside these ranges and needn't reach their ends.
Inputs may be any that keep to these rules, and one draw needn't show every extreme that they name: `node_ids`: each token names 4 different node groups. Within the 256 tokens of one shard, every node group is named by at most 32 tokens, and some node group by exactly 32.
All inputs are finite; a program needn't handle non-finite values.
Results may differ from the reference program's by a relative error of at most 0.0049.
Values may be sent and summed in bfloat16 or wider, within the bound.
No kernel may reach another device: no remote copies, remote signals or barrier semaphores. Data moves between devices by JAX's collectives and lax.ppermute only.
A program may use at most 64 MiB of HBM per device.

```python
import jax
import jax.numpy as jnp
from jax import lax

D = 6144
FF_E = 1024
EXP_DEV = 2
GROUPS = 4
TS = 256
EXPERTS = 128
TOKENS = 4096
CAP = 32
N_NODE = 64
N_LOCAL = 16


def shard_routes(key):
    key_hot, key_rate, key_perm = jax.random.split(key, 3)
    nodes = jnp.arange(N_NODE, dtype=jnp.int32)
    hot = jax.random.randint(key_hot, (), 0, N_NODE)
    rates = jax.random.randint(key_rate, (N_NODE,), 3, 6)
    rates = jnp.where(nodes == hot, 0, rates)
    remain = GROUPS * TS - CAP
    running = jnp.cumsum(rates)
    edges = remain * running // running[-1]
    counts = edges - jnp.concatenate([jnp.zeros((1,), edges.dtype), edges[:-1]])
    counts = jnp.where(nodes == hot, CAP, counts)
    ends = jnp.cumsum(counts)
    places = jnp.arange(GROUPS * TS, dtype=jnp.int32)
    labels = jnp.sum((ends[None, :] <= places[:, None]).astype(jnp.int32), axis=1)
    table = labels.reshape(GROUPS, TS).T
    order = jax.random.permutation(key_perm, TS)
    return table[order].astype(jnp.int32)


def draw_node_ids(key, part):
    key = jax.random.fold_in(key, 11)
    keys = jax.random.split(key, N_LOCAL)
    return jax.vmap(shard_routes)(keys).reshape(TOKENS, GROUPS)


def shard_levels(own_key, dims, cuts, low, largest):
    loudness, own = 1.0, jax.random.fold_in(own_key, 6)
    for axis_at, parts in cuts:
        heights = jnp.exp(jax.random.uniform(jax.random.fold_in(own, axis_at), (parts,), jnp.float32, low / len(cuts), largest / len(cuts)))
        loudness = loudness * jnp.repeat(heights, dims[axis_at] // parts).reshape([-1 if axis == axis_at else 1 for axis in range(len(dims))])
    return loudness


def scatter_about(stream_key, dims, scale, bound, cuts=(), kind=jnp.bfloat16):
    gain = shard_levels(stream_key, dims, cuts, -0.22, 0.18) if cuts else 1.0
    entries = jax.random.normal(stream_key, dims, jnp.float32) * scale * gain
    return jnp.minimum(jnp.maximum(entries, -bound), bound).astype(kind)


def setup_inputs(seed: int = 0) -> dict:
    seeds = jax.random.split(jax.random.key(seed), 6)
    d_out = scatter_about(seeds[0], (TOKENS, D), 0.2, 2.5, ((0, 16), (1, 64)))
    node_ids = draw_node_ids(jax.random.fold_in(seeds[5], 71), 0)
    gates = jnp.clip(0.1 + 0.9 * jax.random.uniform(seeds[2], (N_NODE, N_LOCAL, CAP, EXP_DEV), jnp.float32) ** shard_levels(seeds[2], (N_NODE, N_LOCAL, CAP, EXP_DEV), ((0, 64),), -0.2, 0.2), 0.1, 1.0)
    hidden = scatter_about(seeds[3], (N_NODE, N_LOCAL, CAP, EXP_DEV, FF_E), 0.3, 2.5, ((0, 64), (4, 16)))
    w_down = scatter_about(seeds[4], (EXPERTS, FF_E, D), FF_E ** -0.5, 0.1875, ((0, 64), (1, 16)))
    return dict(d_out=d_out, node_ids=node_ids, gates=gates, hidden=hidden, w_down=w_down)


def slots_of(node_ids):
    member = jnp.any(node_ids[:, :, None] == jnp.arange(N_NODE, dtype=jnp.int32)[None, None, :], axis=1).astype(jnp.int32)
    member = member.reshape(N_LOCAL, TS, N_NODE)
    before = jnp.cumsum(member, axis=1) - member
    return before.reshape(TOKENS, N_NODE).astype(jnp.int32)


def reference(d_out, node_ids, gates, hidden, w_down):
    slot = slots_of(node_ids)
    slot_pick = jnp.take_along_axis(slot, node_ids, axis=1).astype(jnp.int32)
    shard = (jnp.arange(TOKENS, dtype=jnp.int32) // TS)[:, None]
    flat = ((node_ids * N_LOCAL + shard) * CAP + slot_pick).astype(jnp.int32)
    buffer = jnp.zeros((N_NODE * N_LOCAL * CAP, D), jnp.bfloat16)
    buffer = buffer.at[flat.reshape(-1)].set(jnp.repeat(d_out, GROUPS, axis=0))
    buffer = buffer.reshape(N_NODE, N_LOCAL * CAP, D)
    weights = w_down.reshape(N_NODE, EXP_DEV, FF_E, D)
    saved = hidden.reshape(N_NODE, N_LOCAL * CAP, EXP_DEV, FF_E)
    gating = gates.reshape(N_NODE, N_LOCAL * CAP, EXP_DEV)

    def per_node(items):
        rows, weight, acts, gate = items
        rows_f = rows.astype(jnp.float32)
        upward = jnp.einsum('rd,efd->ref', rows_f, weight.astype(jnp.float32))
        grad_h = (gate[:, :, None] * upward).astype(jnp.bfloat16)
        acts_f = acts.astype(jnp.float32)
        partial_value = jnp.sum(acts_f * upward, axis=-1)
        weighted = (gate[:, :, None] * rows_f[:, None, :]).astype(jnp.bfloat16)
        grad_w = jnp.einsum('ref,red->efd', acts_f, weighted.astype(jnp.float32)).astype(jnp.bfloat16)
        return grad_h, grad_w, partial_value

    grad_h, grad_w, partial_value = lax.map(per_node, (buffer, weights, saved, gating))
    d_hidden = grad_h.reshape(N_NODE, N_LOCAL, CAP, EXP_DEV, FF_E)
    d_down = grad_w.reshape(EXPERTS, FF_E, D)
    partial_value = partial_value.reshape(N_NODE * N_LOCAL * CAP, EXP_DEV)
    d_gates = partial_value[flat.reshape(-1)].reshape(TOKENS, GROUPS, EXP_DEV)
    return d_hidden, d_down, d_gates
```

```python
import functools

import jax
import jax.numpy as jnp
from jax import lax
from jax.experimental import pallas as pl
from jax.experimental.pallas import tpu as pltpu
from jax.sharding import PartitionSpec as P

BF = jnp.bfloat16
F32 = jnp.float32


def dot(a, b, dims=(((1,), (0,)), ((), ()))):
    return lax.dot_general(a, b, dims, preferred_element_type=F32)


def pack_kernel(ids_ref, rows_ref, out_ref):
    groups, toks = ids_ref.shape
    nodes, cap, cols = out_ref.shape
    node = lax.broadcasted_iota(jnp.int32, (nodes, toks), 0)
    member = node == ids_ref[0:1, :]
    for k in range(1, groups):
        member = member | (node == ids_ref[k : k + 1, :])
    earlier = lax.broadcasted_iota(jnp.int32, (toks, toks), 0) < lax.broadcasted_iota(
        jnp.int32, (toks, toks), 1
    )
    before = dot(
        jnp.where(member, 1.0, 0.0).astype(BF), jnp.where(earlier, 1.0, 0.0).astype(BF)
    )
    code = jnp.where(member, before, -1.0).astype(jnp.int32)
    slot = lax.broadcasted_iota(jnp.int32, (nodes, cap, toks), 1)
    placed = jnp.where(code[:, None, :] == slot, 1.0, 0.0).astype(BF)
    out = dot(placed.reshape(nodes * cap, toks), rows_ref[...])
    out_ref[...] = out.astype(BF).reshape(nodes, cap, cols)


def pack(ids, rows, nodes, cap):
    return pl.pallas_call(
        pack_kernel,
        out_shape=jax.ShapeDtypeStruct((nodes, cap, rows.shape[1]), BF),
        compiler_params=pltpu.CompilerParams(vmem_limit_bytes=32 * 1024 * 1024),
        name="pack",
    )(ids, rows)


def up_kernel(rows_ref, w_ref, saved_ref, gate_ref, dh_ref, part_ref, acc_ref):
    step = pl.program_id(0)

    @pl.when(step == 0)
    def _():
        acc_ref[...] = jnp.zeros_like(acc_ref)

    acc_ref[...] += dot(rows_ref[...], w_ref[...], (((1,), (1,)), ((), ())))

    @pl.when(step == pl.num_programs(0) - 1)
    def _():
        up = acc_ref[...]
        dh_ref[...] = (gate_ref[...] * up).astype(BF)
        prod = saved_ref[...].astype(F32) * up
        count, per_dev, cap = part_ref.shape
        width = prod.shape[1] // per_dev
        pick = jnp.where(
            lax.broadcasted_iota(jnp.int32, (8, prod.shape[1]), 0)
            == lax.broadcasted_iota(jnp.int32, (8, prod.shape[1]), 1) // width,
            1.0,
            0.0,
        )
        for at in range(count):
            sums = lax.dot_general(
                pick,
                prod[at * cap : (at + 1) * cap],
                (((1,), (1,)), ((), ())),
                precision=lax.Precision.HIGHEST,
                preferred_element_type=F32,
            )
            part_ref[at] = sums[:per_dev]


def up(rows, w, saved, gate, count, per_dev, tile):
    slots, width = rows.shape
    units = w.shape[0]
    whole = lambda i: (0, 0)
    return pl.pallas_call(
        up_kernel,
        grid=(width // tile,),
        in_specs=[
            pl.BlockSpec((slots, tile), lambda i: (0, i)),
            pl.BlockSpec((units, tile), lambda i: (0, i)),
            pl.BlockSpec((slots, units), whole),
            pl.BlockSpec((slots, units), whole),
        ],
        out_specs=[
            pl.BlockSpec((slots, units), whole),
            pl.BlockSpec((count, per_dev, slots // count), lambda i: (0, 0, 0)),
        ],
        out_shape=[
            jax.ShapeDtypeStruct((slots, units), BF),
            jax.ShapeDtypeStruct((count, per_dev, slots // count), F32),
        ],
        scratch_shapes=[pltpu.VMEM((slots, units), F32)],
        compiler_params=pltpu.CompilerParams(vmem_limit_bytes=32 * 1024 * 1024),
        cost_estimate=pl.CostEstimate(
            flops=2 * slots * units * width,
            bytes_accessed=2 * (slots + units) * width,
            transcendentals=0,
        ),
        name="up",
    )(rows, w, saved, gate)


def down_kernel(hi_ref, lo_ref, rows_ref, out_ref):
    rows = rows_ref[...]
    out_ref[...] = (dot(hi_ref[...], rows) + dot(lo_ref[...], rows)).astype(BF)


def down(hi, lo, rows, tile):
    slots, width = rows.shape
    units = hi.shape[0]
    whole = lambda i: (0, 0)
    return pl.pallas_call(
        down_kernel,
        grid=(width // tile,),
        in_specs=[
            pl.BlockSpec((units, slots), whole),
            pl.BlockSpec((units, slots), whole),
            pl.BlockSpec((slots, tile), lambda i: (0, i)),
        ],
        out_specs=pl.BlockSpec((units, tile), lambda i: (0, i)),
        out_shape=jax.ShapeDtypeStruct((units, width), BF),
        compiler_params=pltpu.CompilerParams(vmem_limit_bytes=32 * 1024 * 1024),
        cost_estimate=pl.CostEstimate(
            flops=4 * slots * units * width,
            bytes_accessed=2 * (slots + units) * width,
            transcendentals=0,
        ),
        name="down",
    )(hi, lo, rows)


def look_kernel(ids_ref, slot_ref, table_ref, out_ref):
    toks, groups = ids_ref.shape
    nodes, wide = table_ref.shape
    per_dev = out_ref.shape[1] // groups
    cap = wide // per_dev
    table = table_ref[...]
    node = lax.broadcasted_iota(jnp.int32, (toks, nodes), 1)
    lane = lax.broadcasted_iota(jnp.int32, (toks, wide), 1)
    found = []
    for k in range(groups):
        hot = jnp.where(ids_ref[:, k : k + 1] == node, 1.0, 0.0)
        line = lax.dot_general(
            hot,
            table,
            (((1,), (0,)), ((), ())),
            precision=lax.Precision.HIGHEST,
            preferred_element_type=F32,
        )
        for j in range(per_dev):
            mine = lane == slot_ref[:, k : k + 1] + j * cap
            found.append(jnp.sum(jnp.where(mine, line, 0.0), axis=1, keepdims=True))
    out_ref[...] = jnp.concatenate(found, axis=1)


def look(ids, slot, table, per_dev):
    return pl.pallas_call(
        look_kernel,
        out_shape=jax.ShapeDtypeStruct((ids.shape[0], ids.shape[1] * per_dev), F32),
        compiler_params=pltpu.CompilerParams(vmem_limit_bytes=32 * 1024 * 1024),
        name="look",
    )(ids, slot, table)


def slots_of(ids, nodes):
    picked = ids[:, :, None] == jnp.arange(nodes, dtype=jnp.int32)[None, None, :]
    member = jnp.any(picked, axis=1).astype(jnp.int32)
    before = jnp.cumsum(member, axis=0) - member
    return jnp.sum(picked.astype(jnp.int32) * before[:, None, :], axis=2)


def largest_tile(width, most):
    return max(t for t in range(128, most + 1, 128) if width % t == 0)


def per_device(d_out, node_ids, gates, hidden, w_down):
    nodes = lax.axis_size("node")
    local = lax.axis_size("local")
    cap, per_dev = gates.shape[2:]
    units = hidden.shape[4]
    width = d_out.shape[1] * nodes
    tile = largest_tile(width, 1024)

    packed = pack(node_ids.T, d_out, nodes, cap)
    arrived = lax.all_to_all(packed, "node", split_axis=0, concat_axis=2, tiled=True)
    arrived = arrived.reshape(cap, width)
    rows = lax.all_gather(arrived, "local", axis=0, tiled=True)

    slot = slots_of(node_ids, nodes)
    saved = hidden.reshape(local * cap, per_dev * units)
    gate = jnp.broadcast_to(
        gates.reshape(local * cap, per_dev, 1), (local * cap, per_dev, units)
    ).reshape(local * cap, per_dev * units)
    scaled = (saved.astype(F32) * gate).T
    hi = scaled.astype(BF)
    lo = (scaled - hi.astype(F32)).astype(BF)

    w = w_down.reshape(per_dev * units, width)
    grad_h, part = up(rows, w, saved, gate, local, per_dev, tile)
    got = lax.all_to_all(part, "local", split_axis=0, concat_axis=0, tiled=True)
    own = jnp.sum(got, axis=0)
    table = lax.all_to_all(
        jnp.broadcast_to(own[None], (nodes, per_dev, cap)),
        "node",
        split_axis=0,
        concat_axis=0,
        tiled=True,
    )
    grad_w = down(hi, lo, rows, tile)
    d_gates = look(node_ids, slot, table.reshape(nodes, per_dev * cap), per_dev)
    return (
        grad_h.reshape(1, local, cap, per_dev, units),
        grad_w.reshape(per_dev, units, width),
        d_gates.reshape(node_ids.shape + (per_dev,)),
    )


def solution(mesh):
    return jax.shard_map(
        per_device,
        mesh=mesh,
        in_specs=(
            P("local", "node"),
            P("local", None),
            P("node", None, None, None),
            P("node", None, None, None, "local"),
            P("node", "local", None),
        ),
        out_specs=(
            P("node", None, None, None, "local"),
            P("node", "local", None),
            P("local", None, None),
        ),
        check_vma=False,
    )
```

```python
import functools

import jax
import jax.numpy as jnp
from jax import lax
from jax.experimental import pallas as pl
from jax.experimental.pallas import tpu as pltpu
from jax.sharding import PartitionSpec as P

BF = jnp.bfloat16
F32 = jnp.float32
VMEM = 16 * 1024 * 1024


def dot(a, b, dims=(((1,), (0,)), ((), ()))):
    return lax.dot_general(a, b, dims, preferred_element_type=F32)


def pack_kernel(ids_ref, rows_ref, out_ref, slot_ref):
    groups, toks = ids_ref.shape
    nodes, cap, cols = out_ref.shape
    node = lax.broadcasted_iota(jnp.int32, (nodes, toks), 0)
    picked = [node == ids_ref[k : k + 1, :] for k in range(groups)]
    member = picked[0]
    for k in range(1, groups):
        member = member | picked[k]
    earlier = lax.broadcasted_iota(jnp.int32, (toks, toks), 0) < lax.broadcasted_iota(
        jnp.int32, (toks, toks), 1
    )
    before = dot(
        jnp.where(member, 1.0, 0.0).astype(BF), jnp.where(earlier, 1.0, 0.0).astype(BF)
    )
    code = jnp.where(member, before, -1.0).astype(jnp.int32)
    slot = lax.broadcasted_iota(jnp.int32, (nodes, cap, toks), 1)
    placed = jnp.where(code[:, None, :] == slot, 1.0, 0.0).astype(BF)
    out = dot(placed.reshape(nodes * cap, toks), rows_ref[...])
    out_ref[...] = out.astype(BF).reshape(nodes, cap, cols)
    for k in range(groups):
        mine = jnp.sum(jnp.where(picked[k], before, 0.0), axis=0, keepdims=True)
        slot_ref[k : k + 1, :] = mine.astype(jnp.int32)


def pack(ids, rows, nodes, cap):
    return pl.pallas_call(
        pack_kernel,
        out_shape=[
            jax.ShapeDtypeStruct((nodes, cap, rows.shape[1]), BF),
            jax.ShapeDtypeStruct(ids.shape, jnp.int32),
        ],
        compiler_params=pltpu.CompilerParams(vmem_limit_bytes=VMEM),
        name="pack",
    )(ids, rows)


def scale_kernel(shard_ref, saved_ref, gate_ref, hi_ref, lo_ref):
    shards, cap, wide = saved_ref.shape
    per_dev = gate_ref.shape[2]
    owner = lax.broadcasted_iota(jnp.int32, (cap, wide), 1) // (wide // per_dev)
    for at in range(shards):
        shard = shard_ref[at]
        scaled = saved_ref[shard].astype(F32) * spread(gate_ref[shard], owner)
        hi = scaled.astype(BF)
        hi_ref[at * cap : (at + 1) * cap] = hi
        lo_ref[at * cap : (at + 1) * cap] = (scaled - hi.astype(F32)).astype(BF)


def spread(gates, owner):
    gate = gates[:, 0:1]
    for j in range(1, gates.shape[1]):
        gate = jnp.where(owner == j, gates[:, j : j + 1], gate)
    return gate


def scale(order, saved, gates):
    shards, cap, wide = saved.shape
    vmem = pl.BlockSpec(memory_space=pltpu.VMEM)
    return pl.pallas_call(
        scale_kernel,
        in_specs=[pl.BlockSpec(memory_space=pltpu.SMEM), vmem, vmem],
        out_shape=[jax.ShapeDtypeStruct((shards * cap, wide), BF)] * 2,
        compiler_params=pltpu.CompilerParams(vmem_limit_bytes=VMEM),
        name="scale",
    )(order, saved, gates)


def up_kernel(*refs):
    *row_refs, w_ref, out_ref = refs
    rows = jnp.concatenate([r[...] for r in row_refs], axis=0)
    out_ref[...] = dot(rows, w_ref[...], (((1,), (1,)), ((), ())))


def up(blocks, w):
    slots, (units, width) = sum(b.shape[0] for b in blocks), w.shape
    return pl.pallas_call(
        up_kernel,
        out_shape=jax.ShapeDtypeStruct((slots, units), F32),
        compiler_params=pltpu.CompilerParams(vmem_limit_bytes=VMEM),
        cost_estimate=pl.CostEstimate(
            flops=2 * slots * units * width,
            bytes_accessed=2 * (slots + units) * width,
            transcendentals=0,
        ),
        name="up",
    )(*blocks, w)


def close_kernel(shard_ref, *refs):
    *up_refs, saved_ref, gate_ref, dh_ref, part_ref = refs
    _, per_dev, cap = part_ref.shape
    wide = saved_ref.shape[2]
    pick = jnp.where(
        lax.broadcasted_iota(jnp.int32, (8, wide), 0)
        == lax.broadcasted_iota(jnp.int32, (8, wide), 1) // (wide // per_dev),
        1.0,
        0.0,
    )
    left = lax.broadcasted_iota(jnp.int32, (cap, wide), 1) // (wide // per_dev)
    at = 0
    for ref in up_refs:
        for row in range(0, ref.shape[0], cap):
            shard = shard_ref[at]
            at += 1
            u = ref[row : row + cap, :]
            gate = spread(gate_ref[shard], left)
            dh_ref[shard] = (gate * u).astype(BF)
            sums = lax.dot_general(
                pick,
                saved_ref[shard].astype(F32) * u,
                (((1,), (1,)), ((), ())),
                precision=lax.Precision.HIGHEST,
                preferred_element_type=F32,
            )
            part_ref[shard] = sums[:per_dev]


def close(order, ups, saved, gates):
    shards, cap, per_dev = gates.shape
    vmem = pl.BlockSpec(memory_space=pltpu.VMEM)
    return pl.pallas_call(
        close_kernel,
        in_specs=[pl.BlockSpec(memory_space=pltpu.SMEM)] + [vmem] * (len(ups) + 2),
        out_shape=[
            jax.ShapeDtypeStruct(saved.shape, BF),
            jax.ShapeDtypeStruct((shards, per_dev, cap), F32),
        ],
        compiler_params=pltpu.CompilerParams(vmem_limit_bytes=VMEM),
        name="close",
    )(order, *ups, saved, gates)


def down_kernel(count, hi_ref, lo_ref, *refs):
    row_refs, rest = refs[:count], refs[count:]
    rows = jnp.concatenate([r[...] for r in row_refs], axis=0)
    out_ref = rest[-1]
    total = dot(
        jnp.concatenate([hi_ref[...], lo_ref[...]], axis=0),
        jnp.concatenate([rows, rows], axis=0),
        (((0,), (0,)), ((), ())),
    )
    if len(rest) == 2:
        total = total + rest[0][...]
    out_ref[...] = total.astype(out_ref.dtype)


def down(hi, lo, at, blocks, total, tile, kind):
    units = hi.shape[1]
    slots, width = sum(b.shape[0] for b in blocks), blocks[0].shape[1]
    tiled = lambda i: (0, i)
    mine = pl.BlockSpec((slots, units), lambda i: (at // slots, 0))
    whole = pl.BlockSpec((units, tile), tiled)
    return pl.pallas_call(
        lambda *refs: down_kernel(len(blocks), *refs),
        grid=(width // tile,),
        in_specs=[mine] * 2
        + [pl.BlockSpec((b.shape[0], tile), tiled) for b in blocks]
        + ([] if total is None else [whole]),
        out_specs=whole,
        out_shape=jax.ShapeDtypeStruct((units, width), kind),
        input_output_aliases={2 + len(blocks): 0} if total is not None and total.dtype == kind else {},
        compiler_params=pltpu.CompilerParams(vmem_limit_bytes=VMEM),
        cost_estimate=pl.CostEstimate(
            flops=4 * slots * units * width,
            bytes_accessed=2 * (slots + 4 * units) * width,
            transcendentals=0,
        ),
        name="down",
    )(hi, lo, *blocks, *([] if total is None else [total]))


def look_kernel(ids_ref, slot_ref, table_ref, out_ref):
    toks, groups = ids_ref.shape
    nodes, wide = table_ref.shape
    per_dev = out_ref.shape[1] // groups
    cap = wide // per_dev
    table = table_ref[...]
    node = lax.broadcasted_iota(jnp.int32, (toks, nodes), 1)
    lane = lax.broadcasted_iota(jnp.int32, (toks, wide), 1)
    found = []
    for k in range(groups):
        hot = jnp.where(ids_ref[:, k : k + 1] == node, 1.0, 0.0)
        line = lax.dot_general(
            hot,
            table,
            (((1,), (0,)), ((), ())),
            precision=lax.Precision.HIGHEST,
            preferred_element_type=F32,
        )
        for j in range(per_dev):
            mine = lane == slot_ref[:, k : k + 1] + j * cap
            found.append(jnp.sum(jnp.where(mine, line, 0.0), axis=1, keepdims=True))
    out_ref[...] = jnp.concatenate(found, axis=1)


def look(ids, slot, table, per_dev):
    return pl.pallas_call(
        look_kernel,
        out_shape=jax.ShapeDtypeStruct((ids.shape[0], ids.shape[1] * per_dev), F32),
        compiler_params=pltpu.CompilerParams(vmem_limit_bytes=VMEM),
        name="look",
    )(ids, slot, table)


def largest_tile(width, most):
    return max(t for t in range(128, most + 1, 128) if width % t == 0)


def per_device(d_out, node_ids, gates, hidden, w_down):
    nodes = lax.axis_size("node")
    local = lax.axis_size("local")
    cap, per_dev = gates.shape[2:]
    units = hidden.shape[4]
    width = d_out.shape[1] * nodes
    tile = largest_tile(width, 1024)

    packed, slot = pack(node_ids.T, d_out, nodes, cap)
    w = w_down.reshape(per_dev * units, width)
    saved = hidden.reshape(local, cap, per_dev * units)
    gate = gates.reshape(local, cap, per_dev)
    own_rows = lax.all_to_all(packed, "node", split_axis=0, concat_axis=2, tiled=True).reshape(cap, width)

    steps = local // 2
    right = [(i, (i + 1) % local) for i in range(local)]
    left = [(i, (i - 1) % local) for i in range(local)]
    order = [t for k in range(1, steps) for t in (-k, k)] + [0, steps]
    shards = ((lax.axis_index("local") + jnp.array(order, jnp.int32)) % local).astype(jnp.int32)
    hi, lo = scale(shards, saved, gate)
    block, place = [own_rows], (local - 2) * cap
    ups, total = [], None
    one, other = own_rows, own_rows
    for k in range(1, steps + 1):
        if k == steps:
            one, other = one[: cap // 2], other[cap // 2 :]
        if k > 1:
            one, ups[-1], total = lax.optimization_barrier((one, ups[-1], total))
        one, other = lax.ppermute(one, "local", right), lax.ppermute(other, "local", left)
        ups.append(up(block, w))
        total = down(hi, lo, place, block, total, tile, F32)
        block, place = [one, other], (2 * k - 2) * cap if k < steps else (local - 1) * cap
    ups.append(up(block, w))
    grad_h, part = close(shards, ups[1:-1] + [ups[0], ups[-1]], saved, gate)
    got = lax.all_to_all(part, "local", split_axis=0, concat_axis=0, tiled=True)
    grad_w = down(hi, lo, place, block, total, tile, BF)
    got, grad_w = lax.optimization_barrier((got, grad_w))
    own = jnp.sum(got, axis=0)
    table = lax.all_to_all(
        jnp.broadcast_to(own[None], (nodes, per_dev, cap)),
        "node",
        split_axis=0,
        concat_axis=0,
        tiled=True,
    )
    d_gates = look(node_ids, slot.T, table.reshape(nodes, per_dev * cap), per_dev)
    return (
        grad_h.reshape(1, local, cap, per_dev, units),
        grad_w.reshape(per_dev, units, width),
        d_gates.reshape(node_ids.shape + (per_dev,)),
    )


def solution(mesh):
    return jax.shard_map(
        per_device,
        mesh=mesh,
        in_specs=(
            P("local", "node"),
            P("local", None),
            P("node", None, None, None),
            P("node", None, None, None, "local"),
            P("node", "local", None),
        ),
        out_specs=(
            P("node", None, None, None, "local"),
            P("node", "local", None),
            P("local", None, None),
        ),
        check_vma=False,
    )
```

```python
import functools

import jax
import jax.numpy as jnp
from jax import lax
from jax.experimental import pallas as pl
from jax.experimental.pallas import tpu as pltpu
from jax.sharding import PartitionSpec as P

BF = jnp.bfloat16
F32 = jnp.float32
VMEM = 16 * 1024 * 1024


def dot(a, b, dims=(((1,), (0,)), ((), ()))):
    return lax.dot_general(a, b, dims, preferred_element_type=F32)


CHUNK = 32
FOLD = 128 // CHUNK


def pack_kernel(ids_ref, rows_ref, out_ref, slot_ref):
    groups, toks = ids_ref.shape
    nodes, part, wide = out_ref.shape
    cols = rows_ref.shape[1]
    node = lax.broadcasted_iota(jnp.int32, (nodes, toks), 0)
    picked = [node == ids_ref[k : k + 1, :] for k in range(groups)]
    member = picked[0]
    for k in range(1, groups):
        member = member | picked[k]
    earlier = lax.broadcasted_iota(jnp.int32, (toks, toks), 0) < lax.broadcasted_iota(
        jnp.int32, (toks, toks), 1
    )
    before = dot(
        jnp.where(member, 1.0, 0.0).astype(BF), jnp.where(earlier, 1.0, 0.0).astype(BF)
    )
    code = jnp.where(member, before, -1.0).astype(jnp.int32)
    slot = lax.broadcasted_iota(jnp.int32, (nodes, part, toks), 1)
    col = lax.broadcasted_iota(jnp.int32, (cols, wide), 0)
    place = col // CHUNK * 128 + col % CHUNK
    lane = lax.broadcasted_iota(jnp.int32, (cols, wide), 1)
    rows = rows_ref[...]
    placed, spaced = [], []
    for at in range(FOLD):
        hit = jnp.where(code[:, None, :] == slot + at * part, 1.0, 0.0)
        placed.append(hit.reshape(nodes * part, toks).astype(BF))
        move = jnp.where(lane == place + at * CHUNK, 1.0, 0.0).astype(BF)
        spaced.append(dot(rows, move).astype(BF))
    out = dot(jnp.concatenate(placed, axis=1), jnp.concatenate(spaced, axis=0))
    out_ref[...] = out.reshape(nodes, part, wide).astype(BF)
    for k in range(groups):
        mine = jnp.sum(jnp.where(picked[k], before, 0.0), axis=0, keepdims=True)
        slot_ref[k : k + 1, :] = mine.astype(jnp.int32)


def pack(ids, rows, nodes, cap):
    return pl.pallas_call(
        pack_kernel,
        out_shape=[
            jax.ShapeDtypeStruct((nodes, cap // FOLD, rows.shape[1] * FOLD), BF),
            jax.ShapeDtypeStruct(ids.shape, jnp.int32),
        ],
        compiler_params=pltpu.CompilerParams(vmem_limit_bytes=VMEM),
        name="pack",
    )(ids, rows)


def unpack_kernel(got_ref, rows_ref):
    nodes, part, wide = got_ref.shape
    chunks = wide // 128
    sets = nodes // FOLD
    got = got_ref[...].astype(F32).reshape(sets, FOLD, part, wide)
    row = lax.broadcasted_iota(jnp.int32, (FOLD * 128, FOLD * 128), 0)
    lane = lax.broadcasted_iota(jnp.int32, (FOLD * 128, FOLD * 128), 1)
    to = row // CHUNK % FOLD * 128 + row // 128 * CHUNK + row % CHUNK
    move = jnp.where(lane == to, 1.0, 0.0).astype(BF)
    for tile in range(chunks):
        parts = []
        for at in range(FOLD * tile, FOLD * tile + FOLD):
            node, chunk = divmod(at, chunks)
            piece = got[:, node, :, chunk * 128 : chunk * 128 + 128]
            parts.append(piece.reshape(sets * part, 128).astype(BF))
        out = dot(jnp.concatenate(parts, axis=1), move)
        for m in range(sets):
            rows = out[m * part : (m + 1) * part]
            rows = jnp.concatenate([rows[:, i * 128 : i * 128 + 128] for i in range(FOLD)], axis=0)
            first = (m * chunks + tile) * 128
            rows_ref[:, first : first + 128] = rows.astype(BF)


def unpack(got):
    nodes, part, wide = got.shape
    return pl.pallas_call(
        unpack_kernel,
        out_shape=jax.ShapeDtypeStruct((part * FOLD, nodes * wide // FOLD), BF),
        compiler_params=pltpu.CompilerParams(vmem_limit_bytes=VMEM),
        name="unpack",
    )(got)


def scale_kernel(shard_ref, saved_ref, gate_ref, *out_refs):
    _, cap, wide = saved_ref.shape
    per_dev = gate_ref.shape[2]
    owner = lax.broadcasted_iota(jnp.int32, (cap, wide), 1) // (wide // per_dev)
    at = 0
    for ref in out_refs:
        rows = ref.shape[0] // 2
        for row in range(0, rows, cap):
            shard = shard_ref[at]
            at += 1
            scaled = saved_ref[shard].astype(F32) * spread(gate_ref[shard], owner)
            hi = scaled.astype(BF)
            ref[row : row + cap] = hi
            ref[rows + row : rows + row + cap] = (scaled - hi.astype(F32)).astype(BF)


def spread(gates, owner):
    gate = gates[:, 0:1]
    for j in range(1, gates.shape[1]):
        gate = jnp.where(owner == j, gates[:, j : j + 1], gate)
    return gate


def scale(order, saved, gates, counts):
    _, cap, wide = saved.shape
    vmem = pl.BlockSpec(memory_space=pltpu.VMEM)
    return pl.pallas_call(
        scale_kernel,
        in_specs=[pl.BlockSpec(memory_space=pltpu.SMEM), vmem, vmem],
        out_shape=[jax.ShapeDtypeStruct((2 * n * cap, wide), BF) for n in counts],
        compiler_params=pltpu.CompilerParams(vmem_limit_bytes=VMEM),
        name="scale",
    )(order, saved, gates)


def up_kernel(*refs):
    *row_refs, w_ref, out_ref = refs
    rows = jnp.concatenate([r[...] for r in row_refs], axis=0)
    out_ref[...] = dot(rows, w_ref[...], (((1,), (1,)), ((), ())))


def up(blocks, w):
    slots, (units, width) = sum(b.shape[0] for b in blocks), w.shape
    return pl.pallas_call(
        up_kernel,
        out_shape=jax.ShapeDtypeStruct((slots, units), F32),
        compiler_params=pltpu.CompilerParams(vmem_limit_bytes=VMEM),
        cost_estimate=pl.CostEstimate(
            flops=2 * slots * units * width,
            bytes_accessed=2 * (slots + units) * width,
            transcendentals=0,
        ),
        name="up",
    )(*blocks, w)


def close_kernel(shard_ref, *refs):
    *up_refs, saved_ref, gate_ref, dh_ref, part_ref = refs
    per_dev, cap = gate_ref.shape[2], gate_ref.shape[1]
    wide = saved_ref.shape[2]
    pick = jnp.where(
        lax.broadcasted_iota(jnp.int32, (8, wide), 0)
        == lax.broadcasted_iota(jnp.int32, (8, wide), 1) // (wide // per_dev),
        1.0,
        0.0,
    )
    left = lax.broadcasted_iota(jnp.int32, (cap, wide), 1) // (wide // per_dev)
    at = 0
    for ref in up_refs:
        for row in range(0, ref.shape[0], cap):
            shard = shard_ref[at]
            at += 1
            u = ref[row : row + cap, :]
            gate = spread(gate_ref[shard], left)
            dh_ref[shard] = (gate * u).astype(BF)
            sums = lax.dot_general(
                pick,
                saved_ref[shard].astype(F32) * u,
                (((1,), (1,)), ((), ())),
                precision=lax.Precision.HIGHEST,
                preferred_element_type=F32,
            )
            part_ref[shard] = jnp.concatenate([sums[j : j + 1] for j in range(per_dev)], axis=1)


def close(order, ups, saved, gates):
    shards, cap, per_dev = gates.shape
    vmem = pl.BlockSpec(memory_space=pltpu.VMEM)
    return pl.pallas_call(
        close_kernel,
        in_specs=[pl.BlockSpec(memory_space=pltpu.SMEM)] + [vmem] * (len(ups) + 2),
        out_shape=[
            jax.ShapeDtypeStruct(saved.shape, BF),
            jax.ShapeDtypeStruct((shards, 1, per_dev * cap), F32),
        ],
        compiler_params=pltpu.CompilerParams(vmem_limit_bytes=VMEM),
        name="close",
    )(order, *ups, saved, gates)


def down_kernel(count, scaled_ref, *refs):
    row_refs, rest = refs[:count], refs[count:]
    rows = jnp.concatenate([r[...] for r in row_refs], axis=0)
    out_ref = rest[-1]
    total = dot(
        scaled_ref[...], jnp.concatenate([rows, rows], axis=0), (((0,), (0,)), ((), ()))
    )
    if len(rest) == 2:
        total = total + rest[0][...]
    out_ref[...] = total.astype(out_ref.dtype)


def down(scaled, blocks, total, tile, kind):
    slots, units = scaled.shape
    width = blocks[0].shape[1]
    tiled = lambda i: (0, i)
    whole = pl.BlockSpec((units, tile), tiled)
    return pl.pallas_call(
        lambda *refs: down_kernel(len(blocks), *refs),
        grid=(width // tile,),
        in_specs=[pl.BlockSpec((slots, units), lambda i: (0, 0))]
        + [pl.BlockSpec((b.shape[0], tile), tiled) for b in blocks]
        + ([] if total is None else [whole]),
        out_specs=whole,
        out_shape=jax.ShapeDtypeStruct((units, width), kind),
        input_output_aliases={1 + len(blocks): 0} if total is not None and total.dtype == kind else {},
        compiler_params=pltpu.CompilerParams(vmem_limit_bytes=VMEM),
        cost_estimate=pl.CostEstimate(
            flops=2 * slots * units * width,
            bytes_accessed=(slots + 8 * units) * width,
            transcendentals=0,
        ),
        name="down",
    )(scaled, *blocks, *([] if total is None else [total]))


def total_kernel(got_ref, out_ref):
    out_ref[...] = jnp.broadcast_to(jnp.sum(got_ref[...], axis=0, keepdims=True), out_ref.shape)


def total_for(got, nodes):
    return pl.pallas_call(
        total_kernel, out_shape=jax.ShapeDtypeStruct((nodes,) + got.shape[1:], F32), name="total"
    )(got)


def look_kernel(ids_ref, slot_ref, table_ref, out_ref):
    groups, toks = ids_ref.shape
    nodes, _, wide = table_ref.shape
    per_dev = out_ref.shape[0] // groups
    cap = wide // per_dev
    node = lax.broadcasted_iota(jnp.int32, (nodes, toks), 0)
    hot = [jnp.where(node == ids_ref[k : k + 1, :], 1.0, 0.0) for k in range(groups)]
    lines = lax.dot_general(
        table_ref[:, 0, :],
        jnp.concatenate(hot, axis=1),
        (((0,), (0,)), ((), ())),
        precision=lax.Precision.HIGHEST,
        preferred_element_type=F32,
    )
    row = lax.broadcasted_iota(jnp.int32, (cap, toks), 0)
    for k in range(groups):
        mine = row == slot_ref[k : k + 1, :]
        for j in range(per_dev):
            part = lines[j * cap : (j + 1) * cap, k * toks : (k + 1) * toks]
            out_ref[k * per_dev + j : k * per_dev + j + 1, :] = jnp.sum(
                jnp.where(mine, part, 0.0), axis=0, keepdims=True
            )


def look(ids, slot, table, per_dev):
    return pl.pallas_call(
        look_kernel,
        out_shape=jax.ShapeDtypeStruct((ids.shape[0] * per_dev, ids.shape[1]), F32),
        compiler_params=pltpu.CompilerParams(vmem_limit_bytes=VMEM),
        name="look",
    )(ids, slot, table)


def largest_tile(width, most):
    return max(t for t in range(128, most + 1, 128) if width % t == 0)


def per_device(d_out, node_ids, gates, hidden, w_down):
    nodes = lax.axis_size("node")
    local = lax.axis_size("local")
    cap, per_dev = gates.shape[2:]
    units = hidden.shape[4]
    width = d_out.shape[1] * nodes
    tile = largest_tile(width, 1024)

    ids = node_ids.T
    packed, slot = pack(ids, d_out, nodes, cap)
    w = w_down.reshape(per_dev * units, width)
    saved = hidden.reshape(local, cap, per_dev * units)
    gate = gates.reshape(local, cap, per_dev)
    own_rows = unpack(lax.all_to_all(packed, "node", split_axis=0, concat_axis=0, tiled=True))

    steps = local // 2
    right = [(i, (i + 1) % local) for i in range(local)]
    left = [(i, (i - 1) % local) for i in range(local)]
    away = [[0]] + [[-k, k] for k in range(1, steps)] + [[steps]]
    order = jnp.array([t for step in away for t in step], jnp.int32)
    shards = ((lax.axis_index("local") + order) % local).astype(jnp.int32)
    groups = [range(k, min(k + 2, steps)) for k in range(0, steps, 2)] + [range(steps, steps + 1)]
    scaled = scale(shards, saved, gate, [sum(len(away[k]) for k in group) for group in groups])
    blocks, ups, total = [[own_rows]], [], None

    def add(at, kind):
        return down(scaled[at], [b for k in groups[at] for b in blocks[k]], total, tile, kind)

    one, other = own_rows, own_rows
    for k in range(1, steps + 1):
        if k == steps:
            one, other = one[: cap // 2], other[cap // 2 :]
        if k > 1:
            one, ups[-1], total = lax.optimization_barrier((one, ups[-1], total))
        one, other = lax.ppermute(one, "local", right), lax.ppermute(other, "local", left)
        ups.append(up(blocks[-1], w))
        for at, group in enumerate(groups):
            if group[-1] == k - 1:
                total = add(at, F32)
        blocks.append([one, other])
    blocks[-1][1], total = lax.optimization_barrier((blocks[-1][1], total))
    ups.append(up(blocks[-1], w))
    grad_h, part = close(shards, ups, saved, gate)
    got = lax.all_to_all(part, "local", split_axis=0, concat_axis=0, tiled=True)
    table = lax.all_to_all(total_for(got, nodes), "node", split_axis=0, concat_axis=0, tiled=True)
    grad_w = add(len(groups) - 1, BF)
    d_gates = look(ids, slot, table, per_dev)
    return (
        grad_h.reshape(1, local, cap, per_dev, units),
        grad_w.reshape(per_dev, units, width),
        d_gates.reshape(node_ids.shape[1], per_dev, -1).transpose(2, 0, 1),
    )


def solution(mesh):
    return jax.shard_map(
        per_device,
        mesh=mesh,
        in_specs=(
            P("local", "node"),
            P("local", None),
            P("node", None, None, None),
            P("node", None, None, None, "local"),
            P("node", "local", None),
        ),
        out_specs=(
            P("node", None, None, None, "local"),
            P("node", "local", None),
            P("local", None, None),
        ),
        check_vma=False,
    )
```

```python
import functools

import jax
import jax.numpy as jnp
from jax import lax
from jax.experimental import pallas as pl
from jax.experimental.pallas import tpu as pltpu
from jax.sharding import PartitionSpec as P

BF = jnp.bfloat16
F32 = jnp.float32
VMEM = 16 * 1024 * 1024


def dot(a, b, dims=(((1,), (0,)), ((), ()))):
    return lax.dot_general(a, b, dims, preferred_element_type=F32)


CHUNK = 32
FOLD = 128 // CHUNK


def pack_kernel(ids_ref, rows_ref, out_ref, slot_ref):
    groups, toks = ids_ref.shape
    nodes, part, wide = out_ref.shape
    cols = rows_ref.shape[1]
    node = lax.broadcasted_iota(jnp.int32, (nodes, toks), 0)
    picked = [node == ids_ref[k : k + 1, :] for k in range(groups)]
    member = picked[0]
    for k in range(1, groups):
        member = member | picked[k]
    earlier = lax.broadcasted_iota(jnp.int32, (toks, toks), 0) < lax.broadcasted_iota(
        jnp.int32, (toks, toks), 1
    )
    before = dot(
        jnp.where(member, 1.0, 0.0).astype(BF), jnp.where(earlier, 1.0, 0.0).astype(BF)
    )
    code = jnp.where(member, before, -1.0).astype(jnp.int32)
    slot = lax.broadcasted_iota(jnp.int32, (nodes, part, toks), 1)
    col = lax.broadcasted_iota(jnp.int32, (cols, wide), 0)
    place = col // CHUNK * 128 + col % CHUNK
    lane = lax.broadcasted_iota(jnp.int32, (cols, wide), 1)
    rows = rows_ref[...]
    placed, spaced = [], []
    for at in range(FOLD):
        hit = jnp.where(code[:, None, :] == slot + at * part, 1.0, 0.0)
        placed.append(hit.reshape(nodes * part, toks).astype(BF))
        move = jnp.where(lane == place + at * CHUNK, 1.0, 0.0).astype(BF)
        spaced.append(dot(rows, move).astype(BF))
    out = dot(jnp.concatenate(placed, axis=1), jnp.concatenate(spaced, axis=0))
    out_ref[...] = out.reshape(nodes, part, wide).astype(BF)
    for k in range(groups):
        mine = jnp.sum(jnp.where(picked[k], before, 0.0), axis=0, keepdims=True)
        slot_ref[k : k + 1, :] = mine.astype(jnp.int32)


def pack(ids, rows, nodes, cap):
    return pl.pallas_call(
        pack_kernel,
        out_shape=[
            jax.ShapeDtypeStruct((nodes, cap // FOLD, rows.shape[1] * FOLD), BF),
            jax.ShapeDtypeStruct(ids.shape, jnp.int32),
        ],
        compiler_params=pltpu.CompilerParams(vmem_limit_bytes=VMEM),
        name="pack",
    )(ids, rows)


def unpack_kernel(got_ref, rows_ref):
    nodes, part, wide = got_ref.shape
    chunks = wide // 128
    sets = nodes // FOLD
    got = got_ref[...].astype(F32).reshape(sets, FOLD, part, wide)
    row = lax.broadcasted_iota(jnp.int32, (FOLD * 128, FOLD * 128), 0)
    lane = lax.broadcasted_iota(jnp.int32, (FOLD * 128, FOLD * 128), 1)
    to = row // CHUNK % FOLD * 128 + row // 128 * CHUNK + row % CHUNK
    move = jnp.where(lane == to, 1.0, 0.0).astype(BF)
    for tile in range(chunks):
        parts = []
        for at in range(FOLD * tile, FOLD * tile + FOLD):
            node, chunk = divmod(at, chunks)
            piece = got[:, node, :, chunk * 128 : chunk * 128 + 128]
            parts.append(piece.reshape(sets * part, 128).astype(BF))
        out = dot(jnp.concatenate(parts, axis=1), move)
        for m in range(sets):
            rows = out[m * part : (m + 1) * part]
            rows = jnp.concatenate([rows[:, i * 128 : i * 128 + 128] for i in range(FOLD)], axis=0)
            first = (m * chunks + tile) * 128
            rows_ref[:, first : first + 128] = rows.astype(BF)


def unpack(got):
    nodes, part, wide = got.shape
    return pl.pallas_call(
        unpack_kernel,
        out_shape=jax.ShapeDtypeStruct((part * FOLD, nodes * wide // FOLD), BF),
        compiler_params=pltpu.CompilerParams(vmem_limit_bytes=VMEM),
        name="unpack",
    )(got)


def scale_kernel(shard_ref, saved_ref, gate_ref, *out_refs):
    _, cap, wide = saved_ref.shape
    per_dev = gate_ref.shape[2]
    owner = lax.broadcasted_iota(jnp.int32, (cap, wide), 1) // (wide // per_dev)
    at = 0
    for ref in out_refs:
        rows = ref.shape[0] // 2
        for row in range(0, rows, cap):
            shard = shard_ref[at]
            at += 1
            scaled = saved_ref[shard].astype(F32) * spread(gate_ref[shard], owner)
            hi = scaled.astype(BF)
            ref[row : row + cap] = hi
            ref[rows + row : rows + row + cap] = (scaled - hi.astype(F32)).astype(BF)


def spread(gates, owner):
    gate = gates[:, 0:1]
    for j in range(1, gates.shape[1]):
        gate = jnp.where(owner == j, gates[:, j : j + 1], gate)
    return gate


def scale(order, saved, gates, counts):
    _, cap, wide = saved.shape
    vmem = pl.BlockSpec(memory_space=pltpu.VMEM)
    return pl.pallas_call(
        scale_kernel,
        in_specs=[pl.BlockSpec(memory_space=pltpu.SMEM), vmem, vmem],
        out_shape=[jax.ShapeDtypeStruct((2 * n * cap, wide), BF) for n in counts],
        compiler_params=pltpu.CompilerParams(vmem_limit_bytes=VMEM),
        name="scale",
    )(order, saved, gates)


def up_kernel(*refs):
    *row_refs, w_ref, out_ref = refs
    rows = jnp.concatenate([r[...] for r in row_refs], axis=0)
    out_ref[...] = dot(rows, w_ref[...], (((1,), (1,)), ((), ())))


def up(blocks, w):
    slots, (units, width) = sum(b.shape[0] for b in blocks), w.shape
    return pl.pallas_call(
        up_kernel,
        out_shape=jax.ShapeDtypeStruct((slots, units), F32),
        compiler_params=pltpu.CompilerParams(vmem_limit_bytes=VMEM),
        cost_estimate=pl.CostEstimate(
            flops=2 * slots * units * width,
            bytes_accessed=2 * (slots + units) * width,
            transcendentals=0,
        ),
        name="up",
    )(*blocks, w)


def close_kernel(shard_ref, *refs):
    *up_refs, saved_ref, gate_ref, dh_ref, part_ref = refs
    per_dev, cap = gate_ref.shape[2], gate_ref.shape[1]
    wide = saved_ref.shape[2]
    pick = jnp.where(
        lax.broadcasted_iota(jnp.int32, (8, wide), 0)
        == lax.broadcasted_iota(jnp.int32, (8, wide), 1) // (wide // per_dev),
        1.0,
        0.0,
    )
    left = lax.broadcasted_iota(jnp.int32, (cap, wide), 1) // (wide // per_dev)
    at = 0
    for ref in up_refs:
        for row in range(0, ref.shape[0], cap):
            shard = shard_ref[at]
            at += 1
            u = ref[row : row + cap, :]
            gate = spread(gate_ref[shard], left)
            dh_ref[shard] = (gate * u).astype(BF)
            sums = lax.dot_general(
                pick,
                saved_ref[shard].astype(F32) * u,
                (((1,), (1,)), ((), ())),
                precision=lax.Precision.HIGHEST,
                preferred_element_type=F32,
            )
            part_ref[shard] = jnp.concatenate([sums[j : j + 1] for j in range(per_dev)], axis=1)


def close(order, ups, saved, gates):
    shards, cap, per_dev = gates.shape
    vmem = pl.BlockSpec(memory_space=pltpu.VMEM)
    return pl.pallas_call(
        close_kernel,
        in_specs=[pl.BlockSpec(memory_space=pltpu.SMEM)] + [vmem] * (len(ups) + 2),
        out_shape=[
            jax.ShapeDtypeStruct(saved.shape, BF),
            jax.ShapeDtypeStruct((shards, 1, per_dev * cap), F32),
        ],
        compiler_params=pltpu.CompilerParams(vmem_limit_bytes=VMEM),
        name="close",
    )(order, *ups, saved, gates)


def down_kernel(count, scaled_ref, *refs):
    row_refs, rest = refs[:count], refs[count:]
    rows = jnp.concatenate([r[...] for r in row_refs], axis=0)
    out_ref = rest[-1]
    total = dot(
        scaled_ref[...], jnp.concatenate([rows, rows], axis=0), (((0,), (0,)), ((), ()))
    )
    if len(rest) == 2:
        total = total + rest[0][...]
    out_ref[...] = total.astype(out_ref.dtype)


def down(scaled, blocks, total, tile, kind):
    slots, units = scaled.shape
    width = blocks[0].shape[1]
    tiled = lambda i: (0, i)
    whole = pl.BlockSpec((units, tile), tiled)
    return pl.pallas_call(
        lambda *refs: down_kernel(len(blocks), *refs),
        grid=(width // tile,),
        in_specs=[pl.BlockSpec((slots, units), lambda i: (0, 0))]
        + [pl.BlockSpec((b.shape[0], tile), tiled) for b in blocks]
        + ([] if total is None else [whole]),
        out_specs=whole,
        out_shape=jax.ShapeDtypeStruct((units, width), kind),
        input_output_aliases={1 + len(blocks): 0} if total is not None and total.dtype == kind else {},
        compiler_params=pltpu.CompilerParams(vmem_limit_bytes=VMEM),
        cost_estimate=pl.CostEstimate(
            flops=2 * slots * units * width,
            bytes_accessed=(slots + 8 * units) * width,
            transcendentals=0,
        ),
        name="down",
    )(scaled, *blocks, *([] if total is None else [total]))


def total_kernel(got_ref, out_ref):
    out_ref[...] = jnp.broadcast_to(jnp.sum(got_ref[...], axis=0, keepdims=True), out_ref.shape)


def total_for(got, nodes):
    return pl.pallas_call(
        total_kernel, out_shape=jax.ShapeDtypeStruct((nodes,) + got.shape[1:], F32), name="total"
    )(got)


def look_kernel(ids_ref, slot_ref, table_ref, out_ref):
    groups, toks = ids_ref.shape
    nodes, _, wide = table_ref.shape
    per_dev = out_ref.shape[0] // groups
    cap = wide // per_dev
    node = lax.broadcasted_iota(jnp.int32, (nodes, toks), 0)
    hot = [jnp.where(node == ids_ref[k : k + 1, :], 1.0, 0.0) for k in range(groups)]
    lines = lax.dot_general(
        table_ref[:, 0, :],
        jnp.concatenate(hot, axis=1),
        (((0,), (0,)), ((), ())),
        precision=lax.Precision.HIGHEST,
        preferred_element_type=F32,
    )
    row = lax.broadcasted_iota(jnp.int32, (cap, toks), 0)
    for k in range(groups):
        mine = row == slot_ref[k : k + 1, :]
        for j in range(per_dev):
            part = lines[j * cap : (j + 1) * cap, k * toks : (k + 1) * toks]
            out_ref[k * per_dev + j : k * per_dev + j + 1, :] = jnp.sum(
                jnp.where(mine, part, 0.0), axis=0, keepdims=True
            )


def look(ids, slot, table, per_dev):
    return pl.pallas_call(
        look_kernel,
        out_shape=jax.ShapeDtypeStruct((ids.shape[0] * per_dev, ids.shape[1]), F32),
        compiler_params=pltpu.CompilerParams(vmem_limit_bytes=VMEM),
        name="look",
    )(ids, slot, table)


def largest_tile(width, most):
    return max(t for t in range(128, most + 1, 128) if width % t == 0)


def per_device(d_out, node_ids, gates, hidden, w_down):
    nodes = lax.axis_size("node")
    local = lax.axis_size("local")
    cap, per_dev = gates.shape[2:]
    units = hidden.shape[4]
    width = d_out.shape[1] * nodes
    tile = largest_tile(width, 1024)

    ids = node_ids.T
    packed, slot = pack(ids, d_out, nodes, cap)
    w = w_down.reshape(per_dev * units, width)
    saved = hidden.reshape(local, cap, per_dev * units)
    gate = gates.reshape(local, cap, per_dev)
    own_rows = unpack(lax.all_to_all(packed, "node", split_axis=0, concat_axis=0, tiled=True))

    steps = local // 2
    right = [(i, (i + 1) % local) for i in range(local)]
    left = [(i, (i - 1) % local) for i in range(local)]
    away = [[0]] + [[-k, k] for k in range(1, steps)] + [[steps]]
    order = jnp.array([t for step in away for t in step], jnp.int32)
    shards = ((lax.axis_index("local") + order) % local).astype(jnp.int32)
    groups = [range(k, min(k + 2, steps)) for k in range(0, steps, 2)] + [range(steps, steps + 1)]
    scaled = scale(shards, saved, gate, [sum(len(away[k]) for k in group) for group in groups])
    blocks, ups, total = [[own_rows]], [], None

    def add(at, kind):
        return down(scaled[at], [b for k in groups[at] for b in blocks[k]], total, tile, kind)

    one, other = own_rows, own_rows
    for k in range(1, steps + 1):
        if k == steps:
            one, other = one[: cap // 2], other[cap // 2 :]
        if k == 2:
            one, *scaled = lax.optimization_barrier((one, *scaled))
        if k > 1:
            one, ups[-1], total = lax.optimization_barrier((one, ups[-1], total))
            other, ups[-1] = lax.optimization_barrier((other, ups[-1]))
        one, other = lax.ppermute(one, "local", right), lax.ppermute(other, "local", left)
        ups.append(up(blocks[-1], w))
        for at, group in enumerate(groups):
            if group[-1] == k - 1:
                total = add(at, F32)
        blocks.append([one, other])
    blocks[-1][1], total = lax.optimization_barrier((blocks[-1][1], total))
    ups.append(up(blocks[-1], w))
    grad_h, part = close(shards, ups, saved, gate)
    got = lax.all_to_all(part, "local", split_axis=0, concat_axis=0, tiled=True)
    grad_h = grad_h.reshape(1, local, cap, per_dev, units)
    grad_w = add(len(groups) - 1, BF)
    got, grad_w, grad_h = lax.optimization_barrier((got, grad_w, grad_h))
    table = lax.all_to_all(total_for(got, nodes), "node", split_axis=0, concat_axis=0, tiled=True)
    d_gates = look(ids, slot, table, per_dev)
    return (
        grad_h,
        grad_w.reshape(per_dev, units, width),
        d_gates.reshape(node_ids.shape[1], per_dev, -1).transpose(2, 0, 1),
    )


def solution(mesh):
    return jax.shard_map(
        per_device,
        mesh=mesh,
        in_specs=(
            P("local", "node"),
            P("local", None),
            P("node", None, None, None),
            P("node", None, None, None, "local"),
            P("node", "local", None),
        ),
        out_specs=(
            P("node", None, None, None, "local"),
            P("node", "local", None),
            P("local", None, None),
        ),
        check_vma=False,
    )
```

```python
import functools

import jax
import jax.numpy as jnp
from jax import lax
from jax.experimental import pallas as pl
from jax.experimental.pallas import tpu as pltpu
from jax.sharding import PartitionSpec as P

BF = jnp.bfloat16
F32 = jnp.float32
VMEM = 16 * 1024 * 1024


def dot(a, b, dims=(((1,), (0,)), ((), ()))):
    return lax.dot_general(a, b, dims, preferred_element_type=F32)


CHUNK = 32
FOLD = 128 // CHUNK


def pack_kernel(ids_ref, rows_ref, out_ref, slot_ref):
    groups, toks = ids_ref.shape
    nodes, part, wide = out_ref.shape
    cols = rows_ref.shape[1]
    node = lax.broadcasted_iota(jnp.int32, (nodes, toks), 0)
    picked = [node == ids_ref[k : k + 1, :] for k in range(groups)]
    member = picked[0]
    for k in range(1, groups):
        member = member | picked[k]
    earlier = lax.broadcasted_iota(jnp.int32, (toks, toks), 0) < lax.broadcasted_iota(
        jnp.int32, (toks, toks), 1
    )
    before = dot(
        jnp.where(member, 1.0, 0.0).astype(BF), jnp.where(earlier, 1.0, 0.0).astype(BF)
    )
    code = jnp.where(member, before, -1.0).astype(jnp.int32)
    slot = lax.broadcasted_iota(jnp.int32, (nodes, part, toks), 1)
    col = lax.broadcasted_iota(jnp.int32, (cols, wide), 0)
    place = col // CHUNK * 128 + col % CHUNK
    lane = lax.broadcasted_iota(jnp.int32, (cols, wide), 1)
    rows = rows_ref[...]
    placed, spaced = [], []
    for at in range(FOLD):
        hit = jnp.where(code[:, None, :] == slot + at * part, 1.0, 0.0)
        placed.append(hit.reshape(nodes * part, toks).astype(BF))
        move = jnp.where(lane == place + at * CHUNK, 1.0, 0.0).astype(BF)
        spaced.append(dot(rows, move).astype(BF))
    out = dot(jnp.concatenate(placed, axis=1), jnp.concatenate(spaced, axis=0))
    out_ref[...] = out.reshape(nodes, part, wide).astype(BF)
    for k in range(groups):
        mine = jnp.sum(jnp.where(picked[k], before, 0.0), axis=0, keepdims=True)
        slot_ref[k : k + 1, :] = mine.astype(jnp.int32)


def pack(ids, rows, nodes, cap):
    return pl.pallas_call(
        pack_kernel,
        out_shape=[
            jax.ShapeDtypeStruct((nodes, cap // FOLD, rows.shape[1] * FOLD), BF),
            jax.ShapeDtypeStruct(ids.shape, jnp.int32),
        ],
        compiler_params=pltpu.CompilerParams(vmem_limit_bytes=VMEM),
        name="pack",
    )(ids, rows)


def unpack_kernel(got_ref, rows_ref):
    nodes, part, wide = got_ref.shape
    chunks = wide // 128
    sets = nodes // FOLD
    got = got_ref[...].astype(F32).reshape(sets, FOLD, part, wide)
    row = lax.broadcasted_iota(jnp.int32, (FOLD * 128, FOLD * 128), 0)
    lane = lax.broadcasted_iota(jnp.int32, (FOLD * 128, FOLD * 128), 1)
    to = row // CHUNK % FOLD * 128 + row // 128 * CHUNK + row % CHUNK
    move = jnp.where(lane == to, 1.0, 0.0).astype(BF)
    for tile in range(chunks):
        parts = []
        for at in range(FOLD * tile, FOLD * tile + FOLD):
            node, chunk = divmod(at, chunks)
            piece = got[:, node, :, chunk * 128 : chunk * 128 + 128]
            parts.append(piece.reshape(sets * part, 128).astype(BF))
        out = dot(jnp.concatenate(parts, axis=1), move)
        for m in range(sets):
            rows = out[m * part : (m + 1) * part]
            rows = jnp.concatenate([rows[:, i * 128 : i * 128 + 128] for i in range(FOLD)], axis=0)
            first = (m * chunks + tile) * 128
            rows_ref[:, first : first + 128] = rows.astype(BF)


def unpack(got):
    nodes, part, wide = got.shape
    return pl.pallas_call(
        unpack_kernel,
        out_shape=jax.ShapeDtypeStruct((part * FOLD, nodes * wide // FOLD), BF),
        compiler_params=pltpu.CompilerParams(vmem_limit_bytes=VMEM),
        name="unpack",
    )(got)


def scale_kernel(shard_ref, saved_ref, gate_ref, *out_refs):
    _, cap, wide = saved_ref.shape
    per_dev = gate_ref.shape[2]
    owner = lax.broadcasted_iota(jnp.int32, (cap, wide), 1) // (wide // per_dev)
    at = 0
    for ref in out_refs:
        rows = ref.shape[0] // 2
        for row in range(0, rows, cap):
            shard = shard_ref[at]
            at += 1
            scaled = saved_ref[shard].astype(F32) * spread(gate_ref[shard], owner)
            hi = scaled.astype(BF)
            ref[row : row + cap] = hi
            ref[rows + row : rows + row + cap] = (scaled - hi.astype(F32)).astype(BF)


def spread(gates, owner):
    gate = gates[:, 0:1]
    for j in range(1, gates.shape[1]):
        gate = jnp.where(owner == j, gates[:, j : j + 1], gate)
    return gate


def scale(order, saved, gates, counts):
    _, cap, wide = saved.shape
    vmem = pl.BlockSpec(memory_space=pltpu.VMEM)
    return pl.pallas_call(
        scale_kernel,
        in_specs=[pl.BlockSpec(memory_space=pltpu.SMEM), vmem, vmem],
        out_shape=[jax.ShapeDtypeStruct((2 * n * cap, wide), BF) for n in counts],
        compiler_params=pltpu.CompilerParams(vmem_limit_bytes=VMEM),
        name="scale",
    )(order, saved, gates)


def up_kernel(*refs):
    *row_refs, w_ref, out_ref = refs
    rows = jnp.concatenate([r[...] for r in row_refs], axis=0)
    out_ref[...] = dot(rows, w_ref[...], (((1,), (1,)), ((), ())))


def up(blocks, w):
    slots, (units, width) = sum(b.shape[0] for b in blocks), w.shape
    return pl.pallas_call(
        up_kernel,
        out_shape=jax.ShapeDtypeStruct((slots, units), F32),
        compiler_params=pltpu.CompilerParams(vmem_limit_bytes=VMEM),
        cost_estimate=pl.CostEstimate(
            flops=2 * slots * units * width,
            bytes_accessed=2 * (slots + units) * width,
            transcendentals=0,
        ),
        name="up",
    )(*blocks, w)


def close_kernel(shard_ref, *refs):
    *up_refs, saved_ref, gate_ref, dh_ref, part_ref = refs
    per_dev, cap = gate_ref.shape[2], gate_ref.shape[1]
    wide = saved_ref.shape[2]
    pick = jnp.where(
        lax.broadcasted_iota(jnp.int32, (8, wide), 0)
        == lax.broadcasted_iota(jnp.int32, (8, wide), 1) // (wide // per_dev),
        1.0,
        0.0,
    )
    left = lax.broadcasted_iota(jnp.int32, (cap, wide), 1) // (wide // per_dev)
    at = 0
    for ref in up_refs:
        for row in range(0, ref.shape[0], cap):
            shard = shard_ref[at]
            at += 1
            u = ref[row : row + cap, :]
            gate = spread(gate_ref[shard], left)
            dh_ref[shard] = (gate * u).astype(BF)
            sums = lax.dot_general(
                pick,
                saved_ref[shard].astype(F32) * u,
                (((1,), (1,)), ((), ())),
                precision=lax.Precision.HIGHEST,
                preferred_element_type=F32,
            )
            part_ref[shard] = jnp.concatenate([sums[j : j + 1] for j in range(per_dev)], axis=1)


def close(order, ups, saved, gates):
    shards, cap, per_dev = gates.shape
    vmem = pl.BlockSpec(memory_space=pltpu.VMEM)
    return pl.pallas_call(
        close_kernel,
        in_specs=[pl.BlockSpec(memory_space=pltpu.SMEM)] + [vmem] * (len(ups) + 2),
        out_shape=[
            jax.ShapeDtypeStruct(saved.shape, BF),
            jax.ShapeDtypeStruct((shards, 1, per_dev * cap), F32),
        ],
        compiler_params=pltpu.CompilerParams(vmem_limit_bytes=VMEM),
        name="close",
    )(order, *ups, saved, gates)


def down_kernel(count, scaled_ref, *refs):
    row_refs, rest = refs[:count], refs[count:]
    rows = jnp.concatenate([r[...] for r in row_refs], axis=0)
    out_ref = rest[-1]
    total = dot(
        scaled_ref[...], jnp.concatenate([rows, rows], axis=0), (((0,), (0,)), ((), ()))
    )
    if len(rest) == 2:
        total = total + rest[0][...]
    out_ref[...] = total.astype(out_ref.dtype)


def down(scaled, blocks, total, tile, kind):
    slots, units = scaled.shape
    width = blocks[0].shape[1]
    tiled = lambda i: (0, i)
    whole = pl.BlockSpec((units, tile), tiled)
    return pl.pallas_call(
        lambda *refs: down_kernel(len(blocks), *refs),
        grid=(width // tile,),
        in_specs=[pl.BlockSpec((slots, units), lambda i: (0, 0))]
        + [pl.BlockSpec((b.shape[0], tile), tiled) for b in blocks]
        + ([] if total is None else [whole]),
        out_specs=whole,
        out_shape=jax.ShapeDtypeStruct((units, width), kind),
        input_output_aliases={1 + len(blocks): 0} if total is not None and total.dtype == kind else {},
        compiler_params=pltpu.CompilerParams(vmem_limit_bytes=VMEM),
        cost_estimate=pl.CostEstimate(
            flops=2 * slots * units * width,
            bytes_accessed=(slots + 8 * units) * width,
            transcendentals=0,
        ),
        name="down",
    )(scaled, *blocks, *([] if total is None else [total]))


def total_kernel(got_ref, out_ref):
    out_ref[...] = jnp.broadcast_to(jnp.sum(got_ref[...], axis=0, keepdims=True), out_ref.shape)


def total_for(got, nodes):
    return pl.pallas_call(
        total_kernel, out_shape=jax.ShapeDtypeStruct((nodes,) + got.shape[1:], F32), name="total"
    )(got)


def look_kernel(ids_ref, slot_ref, table_ref, out_ref):
    groups, toks = ids_ref.shape
    nodes, _, wide = table_ref.shape
    per_dev = out_ref.shape[0] // groups
    cap = wide // per_dev
    node = lax.broadcasted_iota(jnp.int32, (nodes, toks), 0)
    hot = [jnp.where(node == ids_ref[k : k + 1, :], 1.0, 0.0) for k in range(groups)]
    lines = lax.dot_general(
        table_ref[:, 0, :],
        jnp.concatenate(hot, axis=1),
        (((0,), (0,)), ((), ())),
        precision=lax.Precision.HIGHEST,
        preferred_element_type=F32,
    )
    row = lax.broadcasted_iota(jnp.int32, (cap, toks), 0)
    for k in range(groups):
        mine = row == slot_ref[k : k + 1, :]
        for j in range(per_dev):
            part = lines[j * cap : (j + 1) * cap, k * toks : (k + 1) * toks]
            out_ref[k * per_dev + j : k * per_dev + j + 1, :] = jnp.sum(
                jnp.where(mine, part, 0.0), axis=0, keepdims=True
            )


def look(ids, slot, table, per_dev):
    return pl.pallas_call(
        look_kernel,
        out_shape=jax.ShapeDtypeStruct((ids.shape[0] * per_dev, ids.shape[1]), F32),
        compiler_params=pltpu.CompilerParams(vmem_limit_bytes=VMEM),
        name="look",
    )(ids, slot, table)


def largest_tile(width, most):
    return max(t for t in range(128, most + 1, 128) if width % t == 0)


def per_device(d_out, node_ids, gates, hidden, w_down):
    nodes = lax.axis_size("node")
    local = lax.axis_size("local")
    cap, per_dev = gates.shape[2:]
    units = hidden.shape[4]
    width = d_out.shape[1] * nodes
    tile = largest_tile(width, 1024)

    ids = node_ids.T
    packed, slot = pack(ids, d_out, nodes, cap)
    w = w_down.reshape(per_dev * units, width)
    saved = hidden.reshape(local, cap, per_dev * units)
    gate = gates.reshape(local, cap, per_dev)
    own_rows = unpack(lax.all_to_all(packed, "node", split_axis=0, concat_axis=0, tiled=True))

    steps = local // 2
    right = [(i, (i + 1) % local) for i in range(local)]
    left = [(i, (i - 1) % local) for i in range(local)]
    away = [[0]] + [[-k, k] for k in range(1, steps)] + [[steps]]
    order = jnp.array([t for step in away for t in step], jnp.int32)
    shards = ((lax.axis_index("local") + order) % local).astype(jnp.int32)
    groups = [range(k, min(k + 2, steps)) for k in range(0, steps, 2)] + [range(steps, steps + 1)]
    scaled = scale(shards, saved, gate, [sum(len(away[k]) for k in group) for group in groups])
    blocks, ups, total = [[own_rows]], [], None

    def add(at, kind):
        return down(scaled[at], [b for k in groups[at] for b in blocks[k]], total, tile, kind)

    one, other = own_rows, own_rows
    for k in range(1, steps + 1):
        if k == 2:
            one, *scaled = lax.optimization_barrier((one, *scaled))
        if k > 1:
            one, ups[-1], total = lax.optimization_barrier((one, ups[-1], total))
            other, ups[-1] = lax.optimization_barrier((other, ups[-1]))
        one = lax.ppermute(one, "local", right)
        if k < steps:
            other = lax.ppermute(other, "local", left)
        ups.append(up(blocks[-1], w))
        for at, group in enumerate(groups):
            if group[-1] == k - 1:
                total = add(at, F32)
        blocks.append([one, other] if k < steps else [one])
    blocks[-1][0], total = lax.optimization_barrier((blocks[-1][0], total))
    ups.append(up(blocks[-1], w))
    grad_h, part = close(shards, ups, saved, gate)
    got = lax.all_to_all(part, "local", split_axis=0, concat_axis=0, tiled=True)
    grad_h = grad_h.reshape(1, local, cap, per_dev, units)
    grad_w = add(len(groups) - 1, BF)
    got, grad_w, grad_h = lax.optimization_barrier((got, grad_w, grad_h))
    table = lax.all_to_all(total_for(got, nodes), "node", split_axis=0, concat_axis=0, tiled=True)
    d_gates = look(ids, slot, table, per_dev)
    return (
        grad_h,
        grad_w.reshape(per_dev, units, width),
        d_gates.reshape(node_ids.shape[1], per_dev, -1).transpose(2, 0, 1),
    )


def solution(mesh):
    return jax.shard_map(
        per_device,
        mesh=mesh,
        in_specs=(
            P("local", "node"),
            P("local", None),
            P("node", None, None, None),
            P("node", None, None, None, "local"),
            P("node", "local", None),
        ),
        out_specs=(
            P("node", None, None, None, "local"),
            P("node", "local", None),
            P("local", None, None),
        ),
        check_vma=False,
    )
```

```python
import functools

import jax
import jax.numpy as jnp
from jax import lax
from jax.experimental import pallas as pl
from jax.experimental.pallas import tpu as pltpu
from jax.sharding import PartitionSpec as P

BF = jnp.bfloat16
F32 = jnp.float32
VMEM = 16 * 1024 * 1024


def dot(a, b, dims=(((1,), (0,)), ((), ()))):
    return lax.dot_general(a, b, dims, preferred_element_type=F32)


CHUNK = 32
FOLD = 128 // CHUNK


def pack_kernel(ids_ref, rows_ref, out_ref, slot_ref):
    groups, toks = ids_ref.shape
    nodes, part, wide = out_ref.shape
    cols = rows_ref.shape[1]
    node = lax.broadcasted_iota(jnp.int32, (nodes, toks), 0)
    picked = [node == ids_ref[k : k + 1, :] for k in range(groups)]
    member = picked[0]
    for k in range(1, groups):
        member = member | picked[k]
    earlier = lax.broadcasted_iota(jnp.int32, (toks, toks), 0) < lax.broadcasted_iota(
        jnp.int32, (toks, toks), 1
    )
    before = dot(
        jnp.where(member, 1.0, 0.0).astype(BF), jnp.where(earlier, 1.0, 0.0).astype(BF)
    )
    code = jnp.where(member, before, -1.0).astype(jnp.int32)
    slot = lax.broadcasted_iota(jnp.int32, (nodes, part, toks), 1)
    col = lax.broadcasted_iota(jnp.int32, (cols, wide), 0)
    place = col // CHUNK * 128 + col % CHUNK
    lane = lax.broadcasted_iota(jnp.int32, (cols, wide), 1)
    rows = rows_ref[...]
    placed, spaced = [], []
    for at in range(FOLD):
        hit = jnp.where(code[:, None, :] == slot + at * part, 1.0, 0.0)
        placed.append(hit.reshape(nodes * part, toks).astype(BF))
        move = jnp.where(lane == place + at * CHUNK, 1.0, 0.0).astype(BF)
        spaced.append(dot(rows, move).astype(BF))
    out = dot(jnp.concatenate(placed, axis=1), jnp.concatenate(spaced, axis=0))
    out_ref[...] = out.reshape(nodes, part, wide).astype(BF)
    for k in range(groups):
        mine = jnp.sum(jnp.where(picked[k], before, 0.0), axis=0, keepdims=True)
        slot_ref[k : k + 1, :] = mine.astype(jnp.int32)


def pack(ids, rows, nodes, cap):
    return pl.pallas_call(
        pack_kernel,
        out_shape=[
            jax.ShapeDtypeStruct((nodes, cap // FOLD, rows.shape[1] * FOLD), BF),
            jax.ShapeDtypeStruct(ids.shape, jnp.int32),
        ],
        compiler_params=pltpu.CompilerParams(vmem_limit_bytes=VMEM),
        name="pack",
    )(ids, rows)


def unpack_kernel(got_ref, rows_ref):
    nodes, part, wide = got_ref.shape
    chunks = wide // 128
    sets = nodes // FOLD
    got = got_ref[...].astype(F32).reshape(sets, FOLD, part, wide)
    row = lax.broadcasted_iota(jnp.int32, (FOLD * 128, FOLD * 128), 0)
    lane = lax.broadcasted_iota(jnp.int32, (FOLD * 128, FOLD * 128), 1)
    to = row // CHUNK % FOLD * 128 + row // 128 * CHUNK + row % CHUNK
    move = jnp.where(lane == to, 1.0, 0.0).astype(BF)
    for tile in range(chunks):
        parts = []
        for at in range(FOLD * tile, FOLD * tile + FOLD):
            node, chunk = divmod(at, chunks)
            piece = got[:, node, :, chunk * 128 : chunk * 128 + 128]
            parts.append(piece.reshape(sets * part, 128).astype(BF))
        out = dot(jnp.concatenate(parts, axis=1), move)
        for m in range(sets):
            rows = out[m * part : (m + 1) * part]
            rows = jnp.concatenate([rows[:, i * 128 : i * 128 + 128] for i in range(FOLD)], axis=0)
            first = (m * chunks + tile) * 128
            rows_ref[:, first : first + 128] = rows.astype(BF)


def unpack(got):
    nodes, part, wide = got.shape
    return pl.pallas_call(
        unpack_kernel,
        out_shape=jax.ShapeDtypeStruct((part * FOLD, nodes * wide // FOLD), BF),
        compiler_params=pltpu.CompilerParams(vmem_limit_bytes=VMEM),
        name="unpack",
    )(got)


def scale_kernel(shard_ref, saved_ref, gate_ref, *out_refs):
    _, cap, wide = saved_ref.shape
    per_dev = gate_ref.shape[2]
    owner = lax.broadcasted_iota(jnp.int32, (cap, wide), 1) // (wide // per_dev)
    at = 0
    for ref in out_refs:
        rows = ref.shape[0] // 2
        for row in range(0, rows, cap):
            shard = shard_ref[at]
            at += 1
            scaled = saved_ref[shard].astype(F32) * spread(gate_ref[shard], owner)
            hi = scaled.astype(BF)
            ref[row : row + cap] = hi
            ref[rows + row : rows + row + cap] = (scaled - hi.astype(F32)).astype(BF)


def spread(gates, owner):
    gate = gates[:, 0:1]
    for j in range(1, gates.shape[1]):
        gate = jnp.where(owner == j, gates[:, j : j + 1], gate)
    return gate


def scale(order, saved, gates, counts):
    _, cap, wide = saved.shape
    vmem = pl.BlockSpec(memory_space=pltpu.VMEM)
    return pl.pallas_call(
        scale_kernel,
        in_specs=[pl.BlockSpec(memory_space=pltpu.SMEM), vmem, vmem],
        out_shape=[jax.ShapeDtypeStruct((2 * n * cap, wide), BF) for n in counts],
        compiler_params=pltpu.CompilerParams(vmem_limit_bytes=VMEM),
        name="scale",
    )(order, saved, gates)


def up_kernel(*refs):
    *row_refs, w_ref, out_ref = refs
    rows = jnp.concatenate([r[...] for r in row_refs], axis=0)
    out_ref[...] = dot(rows, w_ref[...], (((1,), (1,)), ((), ())))


def up(blocks, w):
    slots, (units, width) = sum(b.shape[0] for b in blocks), w.shape
    return pl.pallas_call(
        up_kernel,
        out_shape=jax.ShapeDtypeStruct((slots, units), F32),
        compiler_params=pltpu.CompilerParams(vmem_limit_bytes=VMEM),
        cost_estimate=pl.CostEstimate(
            flops=2 * slots * units * width,
            bytes_accessed=2 * (slots + units) * width,
            transcendentals=0,
        ),
        name="up",
    )(*blocks, w)


def close_kernel(shard_ref, *refs):
    *up_refs, saved_ref, gate_ref, dh_ref, part_ref = refs
    per_dev, cap = gate_ref.shape[2], gate_ref.shape[1]
    wide = saved_ref.shape[2]
    pick = jnp.where(
        lax.broadcasted_iota(jnp.int32, (8, wide), 0)
        == lax.broadcasted_iota(jnp.int32, (8, wide), 1) // (wide // per_dev),
        1.0,
        0.0,
    )
    left = lax.broadcasted_iota(jnp.int32, (cap, wide), 1) // (wide // per_dev)
    at = 0
    for ref in up_refs:
        for row in range(0, ref.shape[0], cap):
            shard = shard_ref[at]
            at += 1
            u = ref[row : row + cap, :]
            gate = spread(gate_ref[shard], left)
            dh_ref[shard] = (gate * u).astype(BF)
            sums = lax.dot_general(
                pick,
                saved_ref[shard].astype(F32) * u,
                (((1,), (1,)), ((), ())),
                precision=lax.Precision.HIGHEST,
                preferred_element_type=F32,
            )
            part_ref[shard] = jnp.concatenate([sums[j : j + 1] for j in range(per_dev)], axis=1)


def close(order, ups, saved, gates):
    shards, cap, per_dev = gates.shape
    vmem = pl.BlockSpec(memory_space=pltpu.VMEM)
    return pl.pallas_call(
        close_kernel,
        in_specs=[pl.BlockSpec(memory_space=pltpu.SMEM)] + [vmem] * (len(ups) + 2),
        out_shape=[
            jax.ShapeDtypeStruct(saved.shape, BF),
            jax.ShapeDtypeStruct((shards, 1, per_dev * cap), F32),
        ],
        compiler_params=pltpu.CompilerParams(vmem_limit_bytes=VMEM),
        name="close",
    )(order, *ups, saved, gates)


def down_kernel(count, scaled_ref, *refs):
    row_refs, rest = refs[:count], refs[count:]
    rows = jnp.concatenate([r[...] for r in row_refs], axis=0)
    out_ref = rest[-1]
    total = dot(
        scaled_ref[...], jnp.concatenate([rows, rows], axis=0), (((0,), (0,)), ((), ()))
    )
    if len(rest) == 2:
        total = total + rest[0][...]
    out_ref[...] = total.astype(out_ref.dtype)


def down(scaled, blocks, total, tile, kind):
    slots, units = scaled.shape
    width = blocks[0].shape[1]
    tiled = lambda i: (0, i)
    whole = pl.BlockSpec((units, tile), tiled)
    return pl.pallas_call(
        lambda *refs: down_kernel(len(blocks), *refs),
        grid=(width // tile,),
        in_specs=[pl.BlockSpec((slots, units), lambda i: (0, 0))]
        + [pl.BlockSpec((b.shape[0], tile), tiled) for b in blocks]
        + ([] if total is None else [whole]),
        out_specs=whole,
        out_shape=jax.ShapeDtypeStruct((units, width), kind),
        input_output_aliases={1 + len(blocks): 0} if total is not None and total.dtype == kind else {},
        compiler_params=pltpu.CompilerParams(vmem_limit_bytes=VMEM),
        cost_estimate=pl.CostEstimate(
            flops=2 * slots * units * width,
            bytes_accessed=(slots + 8 * units) * width,
            transcendentals=0,
        ),
        name="down",
    )(scaled, *blocks, *([] if total is None else [total]))


def total_kernel(got_ref, out_ref):
    out_ref[...] = jnp.broadcast_to(jnp.sum(got_ref[...], axis=0, keepdims=True), out_ref.shape)


def total_for(got, nodes):
    return pl.pallas_call(
        total_kernel, out_shape=jax.ShapeDtypeStruct((nodes,) + got.shape[1:], F32), name="total"
    )(got)


def look_kernel(ids_ref, slot_ref, table_ref, out_ref):
    groups, toks = ids_ref.shape
    nodes, _, wide = table_ref.shape
    per_dev = out_ref.shape[0] // groups
    cap = wide // per_dev
    node = lax.broadcasted_iota(jnp.int32, (nodes, toks), 0)
    hot = [jnp.where(node == ids_ref[k : k + 1, :], 1.0, 0.0) for k in range(groups)]
    lines = lax.dot_general(
        table_ref[:, 0, :],
        jnp.concatenate(hot, axis=1),
        (((0,), (0,)), ((), ())),
        precision=lax.Precision.HIGHEST,
        preferred_element_type=F32,
    )
    row = lax.broadcasted_iota(jnp.int32, (cap, toks), 0)
    for k in range(groups):
        mine = row == slot_ref[k : k + 1, :]
        for j in range(per_dev):
            part = lines[j * cap : (j + 1) * cap, k * toks : (k + 1) * toks]
            out_ref[k * per_dev + j : k * per_dev + j + 1, :] = jnp.sum(
                jnp.where(mine, part, 0.0), axis=0, keepdims=True
            )


def look(ids, slot, table, per_dev):
    return pl.pallas_call(
        look_kernel,
        out_shape=jax.ShapeDtypeStruct((ids.shape[0] * per_dev, ids.shape[1]), F32),
        compiler_params=pltpu.CompilerParams(vmem_limit_bytes=VMEM),
        name="look",
    )(ids, slot, table)


def largest_tile(width, most):
    return max(t for t in range(128, most + 1, 128) if width % t == 0)


def per_device(d_out, node_ids, gates, hidden, w_down):
    nodes = lax.axis_size("node")
    local = lax.axis_size("local")
    cap, per_dev = gates.shape[2:]
    units = hidden.shape[4]
    width = d_out.shape[1] * nodes
    tile = largest_tile(width, 1024)

    ids = node_ids.T
    packed, slot = pack(ids, d_out, nodes, cap)
    w = w_down.reshape(per_dev * units, width)
    saved = hidden.reshape(local, cap, per_dev * units)
    gate = gates.reshape(local, cap, per_dev)
    own_rows = unpack(lax.all_to_all(packed, "node", split_axis=0, concat_axis=0, tiled=True))

    steps = local // 2
    right = [(i, (i + 1) % local) for i in range(local)]
    left = [(i, (i - 1) % local) for i in range(local)]
    away = [[0]] + [[-k, k] for k in range(1, steps)] + [[steps]]
    order = jnp.array([t for step in away for t in step], jnp.int32)
    shards = ((lax.axis_index("local") + order) % local).astype(jnp.int32)
    groups = [range(k, min(k + 2, steps)) for k in range(0, steps, 2)] + [range(steps, steps + 1)]
    scaled = scale(shards, saved, gate, [sum(len(away[k]) for k in group) for group in groups])
    blocks, ups, total = [[own_rows]], [], None

    def add(at, kind):
        return down(scaled[at], [b for k in groups[at] for b in blocks[k]], total, tile, kind)

    one, other = own_rows, own_rows
    for k in range(1, steps + 1):
        if k == 2:
            one, *scaled = lax.optimization_barrier((one, *scaled))
        if k > 1:
            one, ups[-1], total = lax.optimization_barrier((one, ups[-1], total))
            other, ups[-1] = lax.optimization_barrier((other, ups[-1]))
        one = lax.ppermute(one, "local", right)
        if k < steps:
            other = lax.ppermute(other, "local", left)
        ups.append(up(blocks[-1], w))
        for at, group in enumerate(groups):
            if group[-1] == k - 1:
                total = add(at, F32)
        blocks.append([one, other] if k < steps else [one])
    ups[-1], total = lax.optimization_barrier((ups[-1], total))
    ups.append(up(blocks[-1], w))
    grad_h, part = close(shards, ups, saved, gate)
    got = lax.all_to_all(part, "local", split_axis=0, concat_axis=0, tiled=True)
    grad_h = grad_h.reshape(1, local, cap, per_dev, units)
    grad_w = add(len(groups) - 1, BF)
    got, grad_w, grad_h = lax.optimization_barrier((got, grad_w, grad_h))
    table = lax.all_to_all(total_for(got, nodes), "node", split_axis=0, concat_axis=0, tiled=True)
    d_gates = look(ids, slot, table, per_dev)
    return (
        grad_h,
        grad_w.reshape(per_dev, units, width),
        d_gates.reshape(node_ids.shape[1], per_dev, -1).transpose(2, 0, 1),
    )


def solution(mesh):
    return jax.shard_map(
        per_device,
        mesh=mesh,
        in_specs=(
            P("local", "node"),
            P("local", None),
            P("node", None, None, None),
            P("node", None, None, None, "local"),
            P("node", "local", None),
        ),
        out_specs=(
            P("node", None, None, None, "local"),
            P("node", "local", None),
            P("local", None, None),
        ),
        check_vma=False,
    )
```
